32 devices in a mesh: groups: 1, pool: 2 (over core), dev: 16 (over z, y, x).
Axes of the slice: x: 2, y: 2, z: 4, core: 2. Of those that a mesh axis runs over, the one named last changes fastest.
Arguments:
- residual_in: bfloat16 [256, 4096], P(('groups', 'pool', 'dev')), may hold values from -6 to 6
- queries: bfloat16 [256, 8192], P(('groups', 'pool', 'dev')), may hold values from -120 to 120
- key_cache: bfloat16 [256, 128, 512], P(('groups', 'pool', 'dev')), may hold values from -4.5 to 4.5
- value_cache: bfloat16 [256, 128, 512], P(('groups', 'pool', 'dev')), may hold values from -6 to 6
- new_keys: bfloat16 [256, 512], P(('groups', 'pool', 'dev')), may hold values from -4 to 4
- new_values: bfloat16 [256, 512], P(('groups', 'pool', 'dev')), may hold values from -6 to 6
- lengths: int32 [256], P(('groups', 'pool', 'dev')), may hold values from 1 to 128, 16384 in all
- out_weight: bfloat16 [8192, 4096], P('dev'), may hold values from -0.5 to 0.5
- norm_gain: bfloat16 [4096], replicated, may hold values from 0.5 to 1.5
- expert_ids: int32 [256, 8], P(('groups', 'pool', 'dev')), may hold values from 0 to 15, all different within a row; in each aligned block of 8 rows (0 to 7, 8 to 15, ...) at most 4 rows name the same one
- route_weights: float32 [256, 8], P(('groups', 'pool', 'dev')), may hold values from 0.05 to 0.3
- w_gate: bfloat16 [16, 4096, 768], P('dev', None, 'pool'), may hold values from -0.09375 to 0.09375
- w_up: bfloat16 [16, 4096, 768], P('dev', None, 'pool'), may hold values from -0.09375 to 0.09375
- w_down: bfloat16 [16, 768, 4096], P('dev', 'pool'), may hold values from -0.21875 to 0.21875
Outputs:
- layer_out: bfloat16 [256, 4096], P(('groups', 'pool', 'dev'))
The draws below stay inside these ranges and needn't reach their ends.
Inputs may be any that keep to these rules, and one draw needn't show every extreme that they name: `expert_ids`: each row names 8 different experts; within the 8 rows of one device no expert is named more than 4 times, a bound that some block reaches.
All inputs are finite; a program needn't handle non-finite values. No bound on the sum of `lengths` on one device may be relied on, other than what follows from the above.
Results may differ from the reference program's by a relative error of at most 0.008.
Values may be sent and summed in bfloat16 or wider, within the bound.
A program may use at most 64 MiB of HBM per device.

```python
import math
import jax
import jax.numpy as jnp
import numpy as np
from jax import lax

D = 4096
H = 64
KVH = 4
HD = 128
FF = 768
TOPK = 8
R = 8
L = 128
EXPERTS = 16
CAP = 4
ROWS = 256


def clipped_keys(key):
    return jnp.clip(jax.random.normal(key, (ROWS, KVH * HD), jnp.float32), -4.0, 4.0)


def draw_new_keys(key, part):
    shared = clipped_keys(key)
    return shared.astype(jnp.bfloat16)


def draw_key_cache(key, part):
    key = jax.random.fold_in(key, 7)
    cache = jnp.clip(jax.random.normal(key, (ROWS, L, KVH * HD), jnp.float32), -4.0, 4.0)
    return cache.astype(jnp.bfloat16)


def draw_queries(key, part):
    key = jax.random.fold_in(key, 9)
    drawn = jnp.clip(jax.random.normal(key, (ROWS, H, HD), jnp.float32), -4.0, 4.0)
    return drawn.reshape(ROWS, H * HD).astype(jnp.bfloat16)


def block_levels(key, shape, shards, smallest, high):
    level = 1.0
    for position, parts in shards:
        steps = jax.random.uniform(jax.random.fold_in(jax.random.fold_in(key, 6), position), (parts,), jnp.float32, smallest / len(shards), high / len(shards))
        level = level * jnp.repeat(jnp.exp(steps), shape[position] // parts).reshape((-1,) + (1,) * (len(shape) - 1 - position))
    return level


def split_up(count, total, limit, lean):
    weights = [(1 << 20) // math.isqrt(grade ** lean) + 1 for grade in range(2, count + 1)]
    rest, holding = total - limit - (count - 1), [1] * (count - 1)
    while rest > 0:
        candidates = [i for i in range(count - 1) if holding[i] < limit]
        whole, remaining = sum([weights[i] for i in candidates]), rest
        for i in candidates:
            more = min(limit - holding[i], max(1, remaining * weights[i] // whole), rest)
            holding[i] = holding[i] + more
            rest = rest - more
    return np.array([limit] + holding)


def ragged(stream_key, number_of, total, reach, lean):
    if number_of == 2:
        one = jax.random.randint(stream_key, (), max(1, total - reach), min(reach, total - 1) + 1)
        return jnp.stack([one, total - one])
    tallies = jnp.asarray(split_up(number_of, total, reach, lean), jnp.int32)
    couples = (number_of - 1) // 2
    source_of, sink = tallies[1:1 + 2 * couples:2], tallies[2:2 + 2 * couples:2]
    margin = jnp.minimum(source_of - 1, reach - sink)
    shifted = jax.random.randint(jax.random.fold_in(stream_key, 1), (couples,), 0, 1 << 20) % (margin + 1)
    tallies = tallies.at[1:1 + 2 * couples:2].set(source_of - shifted).at[2:2 + 2 * couples:2].set(sink + shifted)
    return tallies[jax.random.permutation(jax.random.fold_in(stream_key, 2), number_of)]


def shared_out(key, own, number, rows, count, top, most, skew):
    order = jax.random.permutation(key, count)
    heavy_load, ordinary = portions_of(count, rows * top, most, skew, True), portions_of(count, rows * top, most, skew, False)
    places = jnp.arange(count)

    def named(sizes, turn):
        used = int((sizes > 0).sum())
        fixed = max(1, used // 4)
        moved = fixed + (places - fixed + turn * (used - fixed)) % max(1, count - fixed)
        return jnp.zeros((count,), jnp.int32).at[order[jnp.where(places < fixed, places, moved)]].set(jnp.asarray(sizes, jnp.int32))

    sizes = jnp.where(number % 4 == 0, named(heavy_load, number // 4), named(ordinary, number - number // 4 - 1))
    mixed = jax.random.permutation(jax.random.fold_in(own, 3), count)
    donor, taker = mixed[0:count // 2 * 2:2], mixed[1:count // 2 * 2:2]
    room = jnp.minimum(sizes[donor] - 1, most - sizes[taker]) // 2
    room = jnp.where((donor == order[0]) | (taker == order[0]) | (sizes[taker] == 0), 0, jnp.maximum(room, 0))
    moved = jax.random.randint(jax.random.fold_in(own, 4), (count // 2,), 0, 1 << 20) % (room + 1)
    sizes = sizes.at[donor].add(-moved).at[taker].add(moved)
    labels = jnp.searchsorted(jnp.cumsum(sizes), jnp.arange(rows * top), side="right").astype(jnp.int32)
    grid = labels.reshape(top, rows).T
    grid = grid[jax.random.permutation(jax.random.fold_in(own, 1), rows)]
    turn = jax.random.randint(jax.random.fold_in(own, 2), (rows, 1), 0, top)
    return jnp.take_along_axis(grid, (jnp.arange(top)[None, :] + turn) % top, axis=1)


def portions_of(number_of, total, most, slope, full):
    portions = [(1 << 20) // math.isqrt(rank ** slope) + 1 for rank in range(1, number_of + 1)]
    largest = most if full else min(most, max(-(-total // number_of), total * portions[0] // sum(portions)))
    least = 1 if total - largest >= number_of - 1 else 0
    given, rest = [largest] + [least] * (number_of - 1), total - largest - least * (number_of - 1)
    while rest > 0:
        free = [i for i in range(1, number_of) if given[i] < largest] or [i for i in range(1, number_of) if given[i] < most]
        whole, left = sum([portions[i] for i in free]), rest
        for i in free:
            more = min(most - given[i], max(1, left * portions[i] // whole), rest)
            given[i] = given[i] + more
            rest = rest - more
    return np.array(given)


def gaussian(key, shape, spread, reach, pieces=(), held_as=jnp.bfloat16):
    array = spread * jax.random.normal(key, shape, jnp.float32)
    if pieces:
        array = array * block_levels(key, shape, pieces, -0.22, 0.18)
    return jnp.clip(array, -reach, reach).astype(held_as)


def setup_inputs(seed: int = 0, part: int = 0) -> dict:
    key_of = jax.random.split(jax.random.key(seed), 15)
    part_splits = jax.random.split(jax.random.fold_in(key_of[14], part), 15)
    residual_in = gaussian(part_splits[0], (ROWS, D), 1.0, 6.0, ((0, 32),))
    queries = draw_queries(jax.random.fold_in(jax.random.fold_in(key_of[14], part), 71), part)
    key_cache = draw_key_cache(jax.random.fold_in(jax.random.fold_in(key_of[14], part), 71), part)
    value_cache = gaussian(part_splits[3], (ROWS, L, KVH * HD), 1.0, 6.0, ((0, 32),))
    new_keys = draw_new_keys(jax.random.fold_in(jax.random.fold_in(key_of[14], part), 71), part)
    new_values = gaussian(part_splits[5], (ROWS, KVH * HD), 1.0, 6.0, ((0, 32),))
    lengths = ragged(part_splits[6], ROWS, ROWS * L // 2, L, 2).astype(jnp.int32)
    out_weight = gaussian(key_of[7], (H * HD, D), HD ** -0.5, 0.5, ((0, 16),))
    norm_gain = jnp.clip(1.0 + 0.1 * jax.random.normal(key_of[8], (D,), jnp.float32), 0.5, 1.5).astype(jnp.bfloat16)
    expert_ids_keys = jax.random.split(jax.random.fold_in(part_splits[9], 1), ROWS // R)
    expert_ids_turns = jax.random.permutation(jax.random.fold_in(part_splits[9], 3), ROWS // R)
    expert_ids = jax.vmap(lambda own, number: shared_out(jax.random.fold_in(part_splits[9], 2), own, number, R, EXPERTS, TOPK, CAP, 2))(expert_ids_keys, expert_ids_turns).reshape((ROWS, TOPK))
    route_weights = jnp.clip(0.05 + 0.25 * jax.random.uniform(part_splits[10], (ROWS, TOPK), jnp.float32) ** block_levels(part_splits[10], (ROWS, TOPK), ((0, 32),), -0.2, 0.2), 0.05, 0.3)
    w_gate = gaussian(key_of[11], (EXPERTS, D, FF), D ** -0.5, 0.09375, ((0, 16), (2, 2)))
    w_up = gaussian(key_of[12], (EXPERTS, D, FF), D ** -0.5, 0.09375, ((0, 16), (2, 2)))
    w_down = gaussian(key_of[13], (EXPERTS, FF, D), FF ** -0.5, 0.21875, ((0, 16), (1, 2)))
    return {"residual_in": residual_in, "queries": queries, "key_cache": key_cache, "value_cache": value_cache, "new_keys": new_keys, "new_values": new_values, "lengths": lengths, "out_weight": out_weight, "norm_gain": norm_gain, "expert_ids": expert_ids, "route_weights": route_weights, "w_gate": w_gate, "w_up": w_up, "w_down": w_down}


def attend(queries, key_cache, value_cache, new_keys, new_values, lengths):
    rows = queries.shape[0]
    span = key_cache.shape[1]
    group = H // KVH
    query_heads = queries.astype(jnp.float32).reshape(rows, KVH, group, HD)
    keys_all = key_cache.astype(jnp.float32).reshape(rows, span, KVH, HD)
    values_all = value_cache.astype(jnp.float32).reshape(rows, span, KVH, HD)
    scale = 1.0 / math.sqrt(HD)
    scores = jnp.einsum('rkgd,rlkd->rkgl', query_heads, keys_all) * scale
    own = jnp.einsum('rkgd,rkd->rkg', query_heads, new_keys.astype(jnp.float32).reshape(rows, KVH, HD)) * scale
    valid = (jnp.arange(span, dtype=jnp.int32)[None, :] < lengths.astype(jnp.int32)[:, None])[:, None, None, :]
    scores = jnp.where(valid, scores, -1e+30)
    top = jnp.maximum(lax.optimization_barrier(jnp.max(scores, axis=-1)), own)
    weights = jnp.where(valid, jnp.exp(scores - top[..., None]), 0.0)
    own_weight = jnp.exp(own - top)
    total = lax.optimization_barrier(jnp.sum(weights, axis=-1)) + own_weight
    weights = (weights / total[..., None]).astype(jnp.bfloat16)
    own_weight = (own_weight / total).astype(jnp.bfloat16)
    mixed = jnp.einsum('rkgl,rlkd->rkgd', weights.astype(jnp.float32), values_all)
    mixed = mixed + own_weight.astype(jnp.float32)[..., None] * new_values.astype(jnp.float32).reshape(rows, KVH, 1, HD)
    return mixed.reshape(rows, H * HD).astype(jnp.bfloat16)

def run_expert(operands):
    block, gate_w, up_w, down_w = operands
    gate_proj = jnp.dot(block, gate_w, preferred_element_type=jnp.float32)
    up_proj = jnp.dot(block, up_w, preferred_element_type=jnp.float32)
    activated = (jax.nn.silu(gate_proj) * up_proj).astype(jnp.bfloat16)
    return jnp.dot(activated, down_w, preferred_element_type=jnp.float32).astype(jnp.bfloat16)

def reference(residual_in, queries, key_cache, value_cache, new_keys, new_values, lengths, out_weight, norm_gain, expert_ids, route_weights, w_gate, w_up, w_down):
    heads_out = attend(queries, key_cache, value_cache, new_keys, new_values, lengths)
    attn_out = jnp.dot(heads_out, out_weight, preferred_element_type=jnp.float32)
    hidden = residual_in.astype(jnp.float32) + attn_out
    mean_square = lax.optimization_barrier(jnp.mean(hidden * hidden, axis=-1, keepdims=True))
    normed = (hidden * lax.rsqrt(mean_square + 1e-06) * norm_gain.astype(jnp.float32)).astype(jnp.bfloat16)
    sources = ROWS // R
    picks = expert_ids.astype(jnp.int32).reshape(sources, R * TOPK)
    onehot = (picks[..., None] == jnp.arange(EXPERTS, dtype=jnp.int32)[None, None, :]).astype(jnp.int32)
    slot = lax.optimization_barrier(jnp.sum((jnp.cumsum(onehot, axis=1) - 1) * onehot, axis=-1))
    anchor = jnp.arange(sources, dtype=jnp.int32)[:, None] * CAP
    place = (picks * (sources * CAP) + anchor + slot).reshape(-1).astype(jnp.int32)
    row_of = (jnp.arange(ROWS * TOPK, dtype=jnp.int32) // TOPK).astype(jnp.int32)
    buffer = jnp.zeros((EXPERTS * sources * CAP, D), jnp.bfloat16).at[place].set(normed[row_of])
    outputs = lax.map(run_expert, (buffer.reshape(EXPERTS, sources * CAP, D), w_gate, w_up, w_down))
    picked = outputs.reshape(EXPERTS * sources * CAP, D)[place].reshape(ROWS, TOPK, D)
    moe = jnp.einsum('rk,rkd->rd', route_weights.astype(jnp.float32), picked.astype(jnp.float32), precision=lax.Precision.HIGHEST)
    return (hidden + moe).astype(jnp.bfloat16)
```

```python
import functools
import math

import jax
import jax.numpy as jnp
from jax import lax
from jax.experimental import pallas as pl
from jax.experimental.pallas import tpu as pltpu
from jax.sharding import PartitionSpec as P

H = 64
KVH = 4
HD = 128
TOPK = 8


def attend(queries, key_cache, value_cache, new_keys, new_values, lengths):
    rows = queries.shape[0]
    span = key_cache.shape[1]
    group = H // KVH
    query_heads = queries.reshape(rows, KVH, group, HD)
    keys_all = key_cache.reshape(rows, span, KVH, HD)
    values_all = value_cache.reshape(rows, span, KVH, HD)
    scale = 1.0 / math.sqrt(HD)
    scores = (
        jnp.einsum("rkgd,rlkd->rkgl", query_heads, keys_all, preferred_element_type=jnp.float32)
        * scale
    )
    own = (
        jnp.einsum(
            "rkgd,rkd->rkg",
            query_heads,
            new_keys.reshape(rows, KVH, HD),
            preferred_element_type=jnp.float32,
        )
        * scale
    )
    valid = (jnp.arange(span, dtype=jnp.int32)[None, :] < lengths[:, None])[:, None, None, :]
    scores = jnp.where(valid, scores, -1e30)
    top = jnp.maximum(jnp.max(scores, axis=-1), own)
    weights = jnp.where(valid, jnp.exp(scores - top[..., None]), 0.0)
    own_weight = jnp.exp(own - top)
    total = jnp.sum(weights, axis=-1) + own_weight
    weights = (weights / total[..., None]).astype(jnp.bfloat16)
    own_weight = (own_weight / total).astype(jnp.bfloat16)
    mixed = jnp.einsum("rkgl,rlkd->rkgd", weights, values_all, preferred_element_type=jnp.float32)
    mixed = mixed + own_weight.astype(jnp.float32)[..., None] * new_values.reshape(
        rows, KVH, 1, HD
    ).astype(jnp.float32)
    return mixed.reshape(rows, H * HD).astype(jnp.bfloat16)


F32 = jnp.float32
BF16 = jnp.bfloat16
ROW = 16


def flip(index, mask):
    for bit in range(mask.bit_length()):
        if (mask >> bit) & 1:
            index = index + (1 << bit) * (1 - 2 * ((index // (1 << bit)) % 2))
    return index


def reverse_bits(value, bits):
    return sum(((value >> bit) & 1) << (bits - 1 - bit) for bit in range(bits))


def layer_kernel(n, *refs):
    bits = n.bit_length() - 1
    tails = bits - 2
    refs = list(refs)

    def take(count):
        taken = refs[:count]
        del refs[:count]
        return taken

    heads, residual, gain, wo_hbm, wg_hbm, wu_hbm, wd_hbm, out = take(8)
    hb, wo, wg, wu, wd, acc, gathered, other, pool_send, pool_recv = take(10)
    res_send, res_recv, sq_send, sq_recv, out_send, out_recv = take(6)
    s1a, s1b, r1a, r1b, s2a, s2b, r2a, r2b = take(8)
    tail_send, tail_recv = take(tails), take(tails)
    local_sem, heads_ss, heads_rs, pool_ss, pool_rs, rs_ss, rs_rs, ag_ss, ag_rs = take(9)

    me = lax.axis_index("dev")
    pool = lax.axis_index("pool")
    mate = {"pool": 1 - pool}
    first = pool == 0
    half = acc.shape[-1]
    quarter = half // 2
    width = wo.shape[0]
    fold = width // 2
    rows = n * ROW

    def remote(source, target, send_sem, recv_sem, device):
        return pltpu.make_async_remote_copy(
            src_ref=source,
            dst_ref=target,
            send_sem=send_sem,
            recv_sem=recv_sem,
            device_id=device,
            device_id_type=pl.DeviceIdType.MESH,
        )

    mine = pl.ds(pl.multiple_of(pool * half, half), half)
    theirs = pl.ds(pl.multiple_of((1 - pool) * half, half), half)
    loads = [
        (wo_hbm.at[:, mine], wo),
        (wg_hbm.at[0, mine], wg.at[0]),
        (wg_hbm.at[0, theirs], wg.at[1]),
        (wu_hbm.at[0, mine], wu.at[0]),
        (wu_hbm.at[0, theirs], wu.at[1]),
        (wd_hbm.at[0, :, mine], wd.at[0]),
        (wd_hbm.at[0, :, theirs], wd.at[1]),
        (heads.at[me], hb.at[pool, 0]),
    ]
    loads = [
        pltpu.make_async_copy(source, target, local_sem.at[i])
        for i, (source, target) in enumerate(loads)
    ]
    for load in (loads[7], loads[0]):
        load.start()

    barrier = pltpu.get_barrier_semaphore()
    pl.semaphore_signal(barrier, inc=1, device_id=mate, device_id_type=pl.DeviceIdType.MESH)
    for j in range(1, n):
        pl.semaphore_signal(
            barrier, inc=1, device_id={"dev": flip(me, j)}, device_id_type=pl.DeviceIdType.MESH
        )
    pl.semaphore_wait(barrier, n)

    sends = []
    for j in range(1, n):
        peer = flip(me, j)
        sends.append(
            remote(
                heads.at[peer],
                hb.at[pool, reverse_bits(j, bits)],
                heads_ss.at[j],
                heads_rs.at[j],
                {"dev": peer},
            )
        )
        sends[-1].start()
    for load in loads[1:7]:
        load.start()

    res = residual[...].astype(F32)
    res_own = jnp.where(first, res[:, :half], res[:, half:])
    res_send[...] = jnp.where(first, res[:, half:], res[:, :half])
    swap_res = remote(res_send, res_recv, pool_ss.at[0], pool_rs.at[0], mate)
    swap_res.start()

    loads[7].wait()
    for send in sends:
        send.wait_recv()
    forward = remote(hb.at[pool], hb.at[pool], pool_ss.at[1], pool_rs.at[1], mate)
    forward.start()
    for send in sends:
        send.wait_send()
    loads[0].wait()
    forward.wait()

    wide = hb[...].astype(F32)
    pairs = jnp.concatenate([wide[0, :, :8], wide[1, :, :8]], axis=1).reshape(rows, -1)
    lower = jnp.concatenate([wide[0, :, 8:], wide[1, :, 8:]], axis=1).reshape(rows, -1)
    left = pairs[:, :fold].astype(BF16)
    right = lower[:, :fold].astype(BF16)
    weight = pairs[:, fold : fold + 1] + pairs[:, fold + 1 : fold + 2]
    step = min(512, half)
    for c in range(0, half, step):
        part = jnp.dot(left, wo[:fold, c : c + step], preferred_element_type=F32) + jnp.dot(
            right, wo[fold:, c : c + step], preferred_element_type=F32
        )
        acc[:, :, :, c : c + step] = part.reshape(2, 2, rows // 4, step)

    def swap(slot, send, recv, mask):
        copy = remote(send, recv, rs_ss.at[slot], rs_rs.at[slot], {"dev": flip(me, mask)})
        copy.start()
        return copy

    def reduce_rows():
        s1a[...] = acc[1, :, :, :quarter].astype(BF16)
        one_a = swap(0, s1a, r1a, 1)
        s1b[...] = acc[:, 1, :, quarter:].astype(BF16)
        one_b = swap(1, s1b, r1b, 2)
        one_a.wait()
        s2a[...] = (acc[0, 1, :, :quarter] + r1a[1].astype(F32)).astype(BF16)
        two_a = swap(2, s2a, r2a, 2)
        one_b.wait()
        s2b[...] = (acc[1, 0, :, quarter:] + r1b[1].astype(F32)).astype(BF16)
        two_b = swap(3, s2b, r2b, 1)
        keep_a = acc[0, 0, :, :quarter] + r1a[0].astype(F32)
        keep_b = acc[0, 0, :, quarter:] + r1b[0].astype(F32)
        two_a.wait()
        two_b.wait()
        keep = jnp.concatenate(
            [keep_a + r2a[...].astype(F32), keep_b + r2b[...].astype(F32)], axis=1
        )
        for t in range(tails):
            count = keep.shape[0] // 2
            tail_send[t][...] = keep[count:].astype(BF16)
            copy = swap(4 + t, tail_send[t], tail_recv[t], 4 << t)
            copy.wait()
            keep = keep[:count] + tail_recv[t][...].astype(F32)
        return keep

    attn = reduce_rows()
    swap_res.wait()
    res_other = res_recv[...]
    hidden = attn + jnp.concatenate(
        [jnp.where(first, res_own, res_other), jnp.where(first, res_other, res_own)], axis=0
    )
    square = jnp.sum(hidden * hidden, axis=1, keepdims=True)
    sq_send[...] = jnp.broadcast_to(square, sq_send.shape)
    swap_sq = remote(sq_send, sq_recv, pool_ss.at[2], pool_rs.at[2], mate)
    swap_sq.start()
    gains = gain[...].astype(F32)
    gains = jnp.where(first, gains[:, :half], gains[:, half:])
    swap_sq.wait()
    mean_square = (square + sq_recv[:, :1]) / (2 * half)
    normed = (hidden * lax.rsqrt(mean_square + 1e-06) * gains).astype(BF16)
    gathered[0, 0, :ROW] = normed

    def gather(slot, view, target, mask):
        copy = remote(view, target, ag_ss.at[slot], ag_rs.at[slot], {"dev": flip(me, mask)})
        copy.start()
        return copy

    passed = []

    def pass_on(slot, index):
        copy = remote(
            gathered.at[index], other.at[index], pool_ss.at[slot], pool_rs.at[slot], mate
        )
        copy.start()
        passed.append(copy)

    count = ROW
    for t in range(tails):
        copy = gather(
            t,
            gathered.at[0, 0, pl.ds(0, count)],
            gathered.at[0, 0, pl.ds(count, count)],
            4 << (tails - 1 - t),
        )
        copy.wait()
        count *= 2
    side_a, side_b = pl.ds(0, quarter), pl.ds(quarter, quarter)
    whole = slice(None)
    one_a = gather(tails, gathered.at[0, 0, :, side_a], gathered.at[0, 1, :, side_a], 2)
    one_b = gather(tails + 1, gathered.at[0, 0, :, side_b], gathered.at[1, 0, :, side_b], 1)
    pass_on(3, (0, 0))
    one_a.wait()
    two_a = gather(tails + 2, gathered.at[0, :, :, side_a], gathered.at[1, :, :, side_a], 1)
    one_b.wait()
    two_b = gather(tails + 3, gathered.at[:, 0, :, side_b], gathered.at[:, 1, :, side_b], 2)
    pass_on(4, (0, 1, whole, side_a))
    pass_on(5, (1, 0, whole, side_b))
    two_a.wait()
    pass_on(6, (1, whole, whole, side_a))
    two_b.wait()
    pass_on(7, (whole, 1, whole, side_b))

    for load in loads[1:7]:
        load.wait()
    own_rows = gathered[...].reshape(rows, half)
    gate_proj = jnp.dot(own_rows, wg[0], preferred_element_type=F32)
    up_proj = jnp.dot(own_rows, wu[0], preferred_element_type=F32)
    for copy in passed:
        copy.wait()
    other_rows = other[...].reshape(rows, half)
    gate_proj = gate_proj + jnp.dot(other_rows, wg[1], preferred_element_type=F32)
    up_proj = up_proj + jnp.dot(other_rows, wu[1], preferred_element_type=F32)
    activated = gate_proj / (1.0 + jnp.exp(-gate_proj)) * up_proj
    activated = (activated * weight).astype(BF16)
    for c in range(0, half, step):
        part = jnp.dot(activated, wd[1, :, c : c + step], preferred_element_type=F32)
        pool_send[:, :, :, c : c + step] = part.astype(BF16).reshape(2, 2, rows // 4, step)
    swap_pool = remote(pool_send, pool_recv, pool_ss.at[8], pool_rs.at[8], mate)
    swap_pool.start()
    for c in range(0, half, step):
        part = jnp.dot(activated, wd[0, :, c : c + step], preferred_element_type=F32)
        acc[:, :, :, c : c + step] = part.reshape(2, 2, rows // 4, step)
    swap_pool.wait()
    acc[...] = acc[...] + pool_recv[...].astype(F32)
    total = hidden + reduce_rows()
    out_send[...] = jnp.where(first, total[8:], total[:8])
    swap_out = remote(out_send, out_recv, pool_ss.at[9], pool_rs.at[9], mate)
    swap_out.start()
    kept = jnp.where(first, total[:8], total[8:])
    swap_out.wait()
    come = out_recv[...]
    out[:, :half] = jnp.where(first, kept, come).astype(BF16)
    out[:, half:] = jnp.where(first, come, kept).astype(BF16)


def local(
    residual_in,
    queries,
    key_cache,
    value_cache,
    new_keys,
    new_values,
    lengths,
    out_weight,
    norm_gain,
    expert_ids,
    route_weights,
    w_gate,
    w_up,
    w_down,
):
    rows, model = residual_in.shape
    n = lax.axis_size("dev")
    bits = n.bit_length() - 1
    width = out_weight.shape[0]
    fold = width // 2
    lanes = (fold + 2 + 127) // 128 * 128
    hidden_units = w_gate.shape[2]
    half = model // 2
    heads_out = attend(queries, key_cache, value_cache, new_keys, new_values, lengths)
    blocks = heads_out.reshape(rows, n, 2, fold).transpose(1, 2, 0, 3).reshape(n, 2 * rows, fold)
    named = expert_ids[:, :, None] == jnp.arange(n, dtype=jnp.int32)[None, None, :]
    dense = jnp.sum(jnp.where(named, route_weights[:, :, None], 0.0), axis=1)
    high = lax.reduce_precision(dense, 8, 7)
    weights = jnp.stack([high, dense - high], axis=-1).astype(BF16).transpose(1, 0, 2)
    weights = jnp.pad(weights, ((0, 0), (0, rows), (0, lanes - fold - 2)))
    heads = jnp.concatenate([blocks, weights], axis=2)

    group = n * ROW // 4
    quarter = half // 2
    first_step = pltpu.VMEM((2, group, quarter), BF16)
    second_step = pltpu.VMEM((group, quarter), BF16)
    tails = [pltpu.VMEM((group >> (t + 1), half), BF16) for t in range(bits - 2)]
    vmem = pl.BlockSpec(memory_space=pltpu.VMEM)
    hbm = pl.BlockSpec(memory_space=pl.ANY)
    dma = pltpu.SemaphoreType.DMA
    return pl.pallas_call(
        functools.partial(layer_kernel, n),
        out_shape=jax.ShapeDtypeStruct((rows, model), BF16),
        in_specs=[hbm, vmem, vmem, hbm, hbm, hbm, hbm],
        out_specs=vmem,
        scratch_shapes=[
            pltpu.VMEM((2, n, ROW, lanes), BF16),
            pltpu.VMEM((width, half), BF16),
            pltpu.VMEM((2, half, hidden_units), BF16),
            pltpu.VMEM((2, half, hidden_units), BF16),
            pltpu.VMEM((2, hidden_units, half), BF16),
            pltpu.VMEM((2, 2, group, half), F32),
            pltpu.VMEM((2, 2, group, half), BF16),
            pltpu.VMEM((2, 2, group, half), BF16),
            pltpu.VMEM((2, 2, group, half), BF16),
            pltpu.VMEM((2, 2, group, half), BF16),
            pltpu.VMEM((rows, half), F32),
            pltpu.VMEM((rows, half), F32),
            pltpu.VMEM((ROW, 128), F32),
            pltpu.VMEM((ROW, 128), F32),
            pltpu.VMEM((rows, half), F32),
            pltpu.VMEM((rows, half), F32),
            first_step,
            first_step,
            first_step,
            first_step,
            second_step,
            second_step,
            second_step,
            second_step,
            *tails,
            *tails,
            dma((8,)),
            dma((n,)),
            dma((n,)),
            dma((10,)),
            dma((10,)),
            dma((bits + 2,)),
            dma((bits + 2,)),
            dma((bits + 2,)),
            dma((bits + 2,)),
        ],
        compiler_params=pltpu.CompilerParams(
            collective_id=0, has_side_effects=True, vmem_limit_bytes=60 * 1024 * 1024
        ),
    )(heads, residual_in, norm_gain.reshape(1, model), out_weight, w_gate, w_up, w_down)


def solution(mesh):
    placed = (
        P(("groups", "pool", "dev"), None),
        P(("groups", "pool", "dev"), None),
        P(("groups", "pool", "dev"), None, None),
        P(("groups", "pool", "dev"), None, None),
        P(("groups", "pool", "dev"), None),
        P(("groups", "pool", "dev"), None),
        P(("groups", "pool", "dev")),
        P("dev", None),
        P(),
        P(("groups", "pool", "dev"), None),
        P(("groups", "pool", "dev"), None),
        P("dev", None, "pool"),
        P("dev", None, "pool"),
        P("dev", "pool", None),
    )
    return jax.shard_map(
        local,
        mesh=mesh,
        in_specs=placed,
        out_specs=P(("groups", "pool", "dev"), None),
        check_vma=False,
    )
```

```python
import functools
import math

import jax
import jax.numpy as jnp
from jax import lax
from jax.experimental import pallas as pl
from jax.experimental.pallas import tpu as pltpu
from jax.sharding import PartitionSpec as P

H = 64
KVH = 4
HD = 128
TOPK = 8


def attend(queries, key_cache, value_cache, new_keys, new_values, lengths):
    rows = queries.shape[0]
    span = key_cache.shape[1]
    group = H // KVH
    query_heads = queries.reshape(rows, KVH, group, HD)
    keys_all = key_cache.reshape(rows, span, KVH, HD)
    values_all = value_cache.reshape(rows, span, KVH, HD)
    scale = 1.0 / math.sqrt(HD)
    scores = (
        jnp.einsum("rkgd,rlkd->rkgl", query_heads, keys_all, preferred_element_type=jnp.float32)
        * scale
    )
    own = (
        jnp.einsum(
            "rkgd,rkd->rkg",
            query_heads,
            new_keys.reshape(rows, KVH, HD),
            preferred_element_type=jnp.float32,
        )
        * scale
    )
    valid = (jnp.arange(span, dtype=jnp.int32)[None, :] < lengths[:, None])[:, None, None, :]
    scores = jnp.where(valid, scores, -1e30)
    top = jnp.maximum(jnp.max(scores, axis=-1), own)
    weights = jnp.where(valid, jnp.exp(scores - top[..., None]), 0.0)
    own_weight = jnp.exp(own - top)
    total = jnp.sum(weights, axis=-1) + own_weight
    weights = (weights / total[..., None]).astype(jnp.bfloat16)
    own_weight = (own_weight / total).astype(jnp.bfloat16)
    mixed = jnp.einsum("rkgl,rlkd->rkgd", weights, values_all, preferred_element_type=jnp.float32)
    mixed = mixed + own_weight.astype(jnp.float32)[..., None] * new_values.reshape(
        rows, KVH, 1, HD
    ).astype(jnp.float32)
    return mixed.reshape(rows, H * HD).astype(jnp.bfloat16)


F32 = jnp.float32
BF16 = jnp.bfloat16
ROW = 16
PIECES = 2


def flip(index, mask):
    for bit in range(mask.bit_length()):
        if (mask >> bit) & 1:
            index = index + (1 << bit) * (1 - 2 * ((index // (1 << bit)) % 2))
    return index


def reverse_bits(value, bits):
    return sum(((value >> bit) & 1) << (bits - 1 - bit) for bit in range(bits))


def layer_kernel(n, *refs):
    bits = n.bit_length() - 1
    tails = bits - 2
    refs = list(refs)

    def take(count):
        taken = refs[:count]
        del refs[:count]
        return taken

    heads, residual, gain, wo_hbm, wg_hbm, wu_hbm, wd_hbm, out = take(8)
    hb, wo, wg, wu, wd, acc, gathered, other, pool_recv = take(9)
    res_send, res_recv, sq_send, sq_recv, out_send, out_recv = take(6)
    s1, r1, s2, r2 = take(4)
    tail_send, tail_recv = take(tails), take(tails)
    local_sem, heads_ss, heads_rs, pool_ss, pool_rs, rs_ss, rs_rs, ag_ss, ag_rs = take(9)
    pass_ss, pass_rs, mix_ss, mix_rs = take(4)

    me = lax.axis_index("dev")
    pool = lax.axis_index("pool")
    mate = {"pool": 1 - pool}
    first = pool == 0
    half = acc.shape[-1]
    quarter = half // 2
    width = wo.shape[0]
    fold = width // 2
    rows = n * ROW

    def remote(source, target, send_sem, recv_sem, device):
        return pltpu.make_async_remote_copy(
            src_ref=source,
            dst_ref=target,
            send_sem=send_sem,
            recv_sem=recv_sem,
            device_id=device,
            device_id_type=pl.DeviceIdType.MESH,
        )

    mine = pl.ds(pl.multiple_of(pool * half, half), half)
    theirs = pl.ds(pl.multiple_of((1 - pool) * half, half), half)
    loads = [
        (wo_hbm.at[:, mine], wo),
        (wg_hbm.at[0, mine], wg.at[0]),
        (wg_hbm.at[0, theirs], wg.at[1]),
        (wu_hbm.at[0, mine], wu.at[0]),
        (wu_hbm.at[0, theirs], wu.at[1]),
        (wd_hbm.at[0, :, mine], wd.at[0]),
        (wd_hbm.at[0, :, theirs], wd.at[1]),
        (heads.at[me], hb.at[pool, 0]),
    ]
    loads = [
        pltpu.make_async_copy(source, target, local_sem.at[i])
        for i, (source, target) in enumerate(loads)
    ]
    for load in (loads[7], loads[0]):
        load.start()

    barrier = pltpu.get_barrier_semaphore()
    pl.semaphore_signal(barrier, inc=1, device_id=mate, device_id_type=pl.DeviceIdType.MESH)
    for j in range(1, n):
        pl.semaphore_signal(
            barrier, inc=1, device_id={"dev": flip(me, j)}, device_id_type=pl.DeviceIdType.MESH
        )
    pl.semaphore_wait(barrier, n)

    sends = []
    for j in range(1, n):
        peer = flip(me, j)
        sends.append(
            remote(
                heads.at[peer],
                hb.at[pool, reverse_bits(j, bits)],
                heads_ss.at[j],
                heads_rs.at[j],
                {"dev": peer},
            )
        )
        sends[-1].start()
    for load in loads[1:7]:
        load.start()

    res = residual[...].astype(F32)
    res_own = jnp.where(first, res[:, :half], res[:, half:])
    res_send[...] = jnp.where(first, res[:, half:], res[:, :half])
    swap_res = remote(res_send, res_recv, pool_ss.at[0], pool_rs.at[0], mate)
    swap_res.start()

    loads[7].wait()
    for send in sends:
        send.wait_recv()
    forward = remote(hb.at[pool], hb.at[pool], pool_ss.at[1], pool_rs.at[1], mate)
    forward.start()
    for send in sends:
        send.wait_send()
    loads[0].wait()
    forward.wait()

    wide = hb[...].astype(F32)
    pairs = jnp.concatenate([wide[0, :, :8], wide[1, :, :8]], axis=1).reshape(rows, -1)
    lower = jnp.concatenate([wide[0, :, 8:], wide[1, :, 8:]], axis=1).reshape(rows, -1)
    left = pairs[:, :fold].astype(BF16)
    right = lower[:, :fold].astype(BF16)
    weight = pairs[:, fold : fold + 1] + pairs[:, fold + 1 : fold + 2]
    chunk = quarter // PIECES
    pieces = []
    for k in range(PIECES):
        pieces.append((0, pl.ds(k * chunk, chunk)))
        pieces.append((1, pl.ds(quarter + k * chunk, chunk)))
    near = [(1, 2), (2, 1)]

    def project(c, cols):
        part = jnp.dot(left, wo[:fold, cols], preferred_element_type=F32) + jnp.dot(
            right, wo[fold:, cols], preferred_element_type=F32
        )
        acc[:, :, :, cols] = part.reshape(2, 2, rows // 4, chunk)

    def reduce_rows(prepare):
        def swap(c, stage, send, recv, mask):
            copy = remote(
                send, recv, rs_ss.at[c, stage], rs_rs.at[c, stage], {"dev": flip(me, mask)}
            )
            copy.start()
            return copy

        flying = []
        for c, (side, cols) in enumerate(pieces):
            prepare(c, cols)
            gone = acc[:, 1, :, cols] if side else acc[1, :, :, cols]
            s1[c] = gone.astype(BF16)
            flying.append(swap(c, 0, s1.at[c], r1.at[c], near[side][0]))
        for c, (side, cols) in enumerate(pieces):
            flying[c].wait()
            gone = acc[1, 0, :, cols] if side else acc[0, 1, :, cols]
            s2[c] = (gone + r1[c, 1].astype(F32)).astype(BF16)
            flying[c] = swap(c, 1, s2.at[c], r2.at[c], near[side][1])
            acc[0, 0, :, cols] = acc[0, 0, :, cols] + r1[c, 0].astype(F32)
        keeps = []
        for t in range(tails + 1):
            for c, (side, cols) in enumerate(pieces):
                flying[c].wait()
                if t == 0:
                    keep = acc[0, 0, :, cols] + r2[c].astype(F32)
                else:
                    count = (rows // 4) >> t
                    keep = acc[0, 0, :count, cols] + tail_recv[t - 1][c].astype(F32)
                if t == tails:
                    keeps.append(keep)
                    continue
                count = (rows // 4) >> (t + 1)
                tail_send[t][c] = keep[count:].astype(BF16)
                flying[c] = swap(c, 2 + t, tail_send[t].at[c], tail_recv[t].at[c], 4 << t)
                acc[0, 0, :count, cols] = keep[:count]
        return jnp.concatenate(keeps[0::2] + keeps[1::2], axis=1)

    attn = reduce_rows(project)
    swap_res.wait()
    res_other = res_recv[...]
    hidden = attn + jnp.concatenate(
        [jnp.where(first, res_own, res_other), jnp.where(first, res_other, res_own)], axis=0
    )
    square = jnp.sum(hidden * hidden, axis=1, keepdims=True)
    sq_send[...] = jnp.broadcast_to(square, sq_send.shape)
    swap_sq = remote(sq_send, sq_recv, pool_ss.at[2], pool_rs.at[2], mate)
    swap_sq.start()
    gains = gain[...].astype(F32)
    gains = jnp.where(first, gains[:, :half], gains[:, half:])
    swap_sq.wait()
    mean_square = (square + sq_recv[:, :1]) / (2 * half)
    normed = (hidden * lax.rsqrt(mean_square + 1e-06) * gains).astype(BF16)
    gathered[0, 0, :ROW] = normed

    def gather(c, stage, view, target, mask):
        copy = remote(view, target, ag_ss.at[c, stage], ag_rs.at[c, stage], {"dev": flip(me, mask)})
        copy.start()
        return copy

    passed = [[] for _ in pieces]

    def pass_on(c, slot, index):
        copy = remote(
            gathered.at[index], other.at[index], pass_ss.at[c, slot], pass_rs.at[c, slot], mate
        )
        copy.start()
        passed[c].append(copy)

    whole = slice(None)
    flying = [None] * len(pieces)
    for t in range(tails):
        count = ROW << t
        for c, (side, cols) in enumerate(pieces):
            if t:
                flying[c].wait()
            flying[c] = gather(
                c,
                t,
                gathered.at[0, 0, pl.ds(0, count), cols],
                gathered.at[0, 0, pl.ds(count, count), cols],
                4 << (tails - 1 - t),
            )
    for c, (side, cols) in enumerate(pieces):
        flying[c].wait()
        flying[c] = gather(
            c,
            tails,
            gathered.at[0, 0, :, cols],
            gathered.at[1, 0, :, cols] if side else gathered.at[0, 1, :, cols],
            near[side][1],
        )
        pass_on(c, 0, (0, 0, whole, cols))
    for c, (side, cols) in enumerate(pieces):
        flying[c].wait()
        flying[c] = gather(
            c,
            tails + 1,
            gathered.at[:, 0, :, cols] if side else gathered.at[0, :, :, cols],
            gathered.at[:, 1, :, cols] if side else gathered.at[1, :, :, cols],
            near[side][0],
        )
        pass_on(c, 1, (1, 0, whole, cols) if side else (0, 1, whole, cols))
    for load in loads[1:7]:
        load.wait()
    gate_proj = jnp.zeros((rows, wg.shape[-1]), F32)
    up_proj = gate_proj
    for c, (side, cols) in enumerate(pieces):
        flying[c].wait()
        pass_on(c, 2, (whole, 1, whole, cols) if side else (1, whole, whole, cols))
        block = gathered[:, :, :, cols].reshape(rows, chunk)
        gate_proj = gate_proj + jnp.dot(block, wg[0, cols], preferred_element_type=F32)
        up_proj = up_proj + jnp.dot(block, wu[0, cols], preferred_element_type=F32)
    for c, (side, cols) in enumerate(pieces):
        for copy in passed[c]:
            copy.wait()
        block = other[:, :, :, cols].reshape(rows, chunk)
        gate_proj = gate_proj + jnp.dot(block, wg[1, cols], preferred_element_type=F32)
        up_proj = up_proj + jnp.dot(block, wu[1, cols], preferred_element_type=F32)
    activated = gate_proj / (1.0 + jnp.exp(-gate_proj)) * up_proj
    activated = (activated * weight).astype(BF16)
    mixes = []
    for c, (side, cols) in enumerate(pieces):
        part = jnp.dot(activated, wd[1, :, cols], preferred_element_type=F32)
        sent = gathered.at[:, :, :, cols]
        sent[...] = part.astype(BF16).reshape(2, 2, rows // 4, chunk)
        mixes.append(remote(sent, pool_recv.at[c], mix_ss.at[c], mix_rs.at[c], mate))
        mixes[-1].start()

    def mix(c, cols):
        part = jnp.dot(activated, wd[0, :, cols], preferred_element_type=F32)
        mixes[c].wait()
        part = part.reshape(2, 2, rows // 4, chunk)
        acc[:, :, :, cols] = part + pool_recv[c].astype(F32)

    total = hidden + reduce_rows(mix)
    out_send[...] = jnp.where(first, total[8:], total[:8])
    swap_out = remote(out_send, out_recv, pool_ss.at[3], pool_rs.at[3], mate)
    swap_out.start()
    kept = jnp.where(first, total[:8], total[8:])
    swap_out.wait()
    come = out_recv[...]
    out[:, :half] = jnp.where(first, kept, come).astype(BF16)
    out[:, half:] = jnp.where(first, come, kept).astype(BF16)


def local(
    residual_in,
    queries,
    key_cache,
    value_cache,
    new_keys,
    new_values,
    lengths,
    out_weight,
    norm_gain,
    expert_ids,
    route_weights,
    w_gate,
    w_up,
    w_down,
):
    rows, model = residual_in.shape
    n = lax.axis_size("dev")
    bits = n.bit_length() - 1
    width = out_weight.shape[0]
    fold = width // 2
    lanes = (fold + 2 + 127) // 128 * 128
    hidden_units = w_gate.shape[2]
    half = model // 2
    heads_out = attend(queries, key_cache, value_cache, new_keys, new_values, lengths)
    blocks = heads_out.reshape(rows, n, 2, fold).transpose(1, 2, 0, 3).reshape(n, 2 * rows, fold)
    named = expert_ids[:, :, None] == jnp.arange(n, dtype=jnp.int32)[None, None, :]
    dense = jnp.sum(jnp.where(named, route_weights[:, :, None], 0.0), axis=1)
    high = lax.reduce_precision(dense, 8, 7)
    weights = jnp.stack([high, dense - high], axis=-1).astype(BF16).transpose(1, 0, 2)
    weights = jnp.pad(weights, ((0, 0), (0, rows), (0, lanes - fold - 2)))
    heads = jnp.concatenate([blocks, weights], axis=2)

    group = n * ROW // 4
    count = 2 * PIECES
    chunk = half // count
    first_step = pltpu.VMEM((count, 2, group, chunk), BF16)
    second_step = pltpu.VMEM((count, group, chunk), BF16)
    tails = [pltpu.VMEM((count, group >> (t + 1), chunk), BF16) for t in range(bits - 2)]
    vmem = pl.BlockSpec(memory_space=pltpu.VMEM)
    hbm = pl.BlockSpec(memory_space=pl.ANY)
    dma = pltpu.SemaphoreType.DMA
    return pl.pallas_call(
        functools.partial(layer_kernel, n),
        out_shape=jax.ShapeDtypeStruct((rows, model), BF16),
        in_specs=[hbm, vmem, vmem, hbm, hbm, hbm, hbm],
        out_specs=vmem,
        scratch_shapes=[
            pltpu.VMEM((2, n, ROW, lanes), BF16),
            pltpu.VMEM((width, half), BF16),
            pltpu.VMEM((2, half, hidden_units), BF16),
            pltpu.VMEM((2, half, hidden_units), BF16),
            pltpu.VMEM((2, hidden_units, half), BF16),
            pltpu.VMEM((2, 2, group, half), F32),
            pltpu.VMEM((2, 2, group, half), BF16),
            pltpu.VMEM((2, 2, group, half), BF16),
            pltpu.VMEM((count, 2, 2, group, chunk), BF16),
            pltpu.VMEM((rows, half), F32),
            pltpu.VMEM((rows, half), F32),
            pltpu.VMEM((ROW, 128), F32),
            pltpu.VMEM((ROW, 128), F32),
            pltpu.VMEM((rows, half), F32),
            pltpu.VMEM((rows, half), F32),
            first_step,
            first_step,
            second_step,
            second_step,
            *tails,
            *tails,
            dma((8,)),
            dma((n,)),
            dma((n,)),
            dma((4,)),
            dma((4,)),
            dma((count, bits)),
            dma((count, bits)),
            dma((count, bits)),
            dma((count, bits)),
            dma((count, 3)),
            dma((count, 3)),
            dma((count,)),
            dma((count,)),
        ],
        compiler_params=pltpu.CompilerParams(
            collective_id=0, has_side_effects=True, vmem_limit_bytes=60 * 1024 * 1024
        ),
    )(heads, residual_in, norm_gain.reshape(1, model), out_weight, w_gate, w_up, w_down)


def solution(mesh):
    placed = (
        P(("groups", "pool", "dev"), None),
        P(("groups", "pool", "dev"), None),
        P(("groups", "pool", "dev"), None, None),
        P(("groups", "pool", "dev"), None, None),
        P(("groups", "pool", "dev"), None),
        P(("groups", "pool", "dev"), None),
        P(("groups", "pool", "dev")),
        P("dev", None),
        P(),
        P(("groups", "pool", "dev"), None),
        P(("groups", "pool", "dev"), None),
        P("dev", None, "pool"),
        P("dev", None, "pool"),
        P("dev", "pool", None),
    )
    return jax.shard_map(
        local,
        mesh=mesh,
        in_specs=placed,
        out_specs=P(("groups", "pool", "dev"), None),
        check_vma=False,
    )
```

```python
import functools
import math

import jax
import jax.numpy as jnp
from jax import lax
from jax.experimental import pallas as pl
from jax.experimental.pallas import tpu as pltpu
from jax.sharding import PartitionSpec as P

H = 64
KVH = 4
HD = 128
TOPK = 8


def attend(queries, key_cache, value_cache, new_keys, new_values, lengths):
    rows = queries.shape[0]
    span = key_cache.shape[1]
    group = H // KVH
    query_heads = queries.reshape(rows, KVH, group, HD)
    keys_all = key_cache.reshape(rows, span, KVH, HD)
    values_all = value_cache.reshape(rows, span, KVH, HD)
    scale = 1.0 / math.sqrt(HD)
    scores = (
        jnp.einsum("rkgd,rlkd->rkgl", query_heads, keys_all, preferred_element_type=jnp.float32)
        * scale
    )
    own = (
        jnp.einsum(
            "rkgd,rkd->rkg",
            query_heads,
            new_keys.reshape(rows, KVH, HD),
            preferred_element_type=jnp.float32,
        )
        * scale
    )
    valid = (jnp.arange(span, dtype=jnp.int32)[None, :] < lengths[:, None])[:, None, None, :]
    scores = jnp.where(valid, scores, -1e30)
    top = jnp.maximum(jnp.max(scores, axis=-1), own)
    weights = jnp.where(valid, jnp.exp(scores - top[..., None]), 0.0)
    own_weight = jnp.exp(own - top)
    total = jnp.sum(weights, axis=-1) + own_weight
    weights = (weights / total[..., None]).astype(jnp.bfloat16)
    own_weight = (own_weight / total).astype(jnp.bfloat16)
    mixed = jnp.einsum("rkgl,rlkd->rkgd", weights, values_all, preferred_element_type=jnp.float32)
    mixed = mixed + own_weight.astype(jnp.float32)[..., None] * new_values.reshape(
        rows, KVH, 1, HD
    ).astype(jnp.float32)
    return mixed.reshape(rows, H * HD).astype(jnp.bfloat16)


F32 = jnp.float32
BF16 = jnp.bfloat16
ROW = 16
PIECES = 2


def flip(index, mask):
    for bit in range(mask.bit_length()):
        if (mask >> bit) & 1:
            index = index + (1 << bit) * (1 - 2 * ((index // (1 << bit)) % 2))
    return index


def reverse_bits(value, bits):
    return sum(((value >> bit) & 1) << (bits - 1 - bit) for bit in range(bits))


def grouped(bits):
    return [(bit, min(2, bits - bit)) for bit in range(2, bits, 2)]


def layer_kernel(n, *refs):
    bits = n.bit_length() - 1
    groups = grouped(bits)
    tails = len(groups)
    refs = list(refs)

    def take(count):
        taken = refs[:count]
        del refs[:count]
        return taken

    heads, residual, gain, wo_hbm, wg_hbm, wu_hbm, wd_hbm, out = take(8)
    hb, wo, wg, wu, wd, acc, gathered, other, pool_recv = take(9)
    res_send, res_recv, sq_send, sq_recv, out_send, out_recv = take(6)
    s1, r1, s2, r2 = take(4)
    tail_send, tail_recv = take(tails), take(tails)
    local_sem, heads_ss, heads_rs, pool_ss, pool_rs, rs_ss, rs_rs, ag_ss, ag_rs = take(9)
    pass_ss, pass_rs, mix_ss, mix_rs = take(4)

    me = lax.axis_index("dev")
    pool = lax.axis_index("pool")
    mate = {"pool": 1 - pool}
    first = pool == 0
    half = acc.shape[-1]
    quarter = half // 2
    width = wo.shape[0]
    fold = width // 2
    rows = n * ROW

    def remote(source, target, send_sem, recv_sem, device):
        return pltpu.make_async_remote_copy(
            src_ref=source,
            dst_ref=target,
            send_sem=send_sem,
            recv_sem=recv_sem,
            device_id=device,
            device_id_type=pl.DeviceIdType.MESH,
        )

    mine = pl.ds(pl.multiple_of(pool * half, half), half)
    theirs = pl.ds(pl.multiple_of((1 - pool) * half, half), half)
    loads = [
        (wo_hbm.at[:, mine], wo),
        (wg_hbm.at[0, mine], wg.at[0]),
        (wg_hbm.at[0, theirs], wg.at[1]),
        (wu_hbm.at[0, mine], wu.at[0]),
        (wu_hbm.at[0, theirs], wu.at[1]),
        (wd_hbm.at[0, :, mine], wd.at[0]),
        (wd_hbm.at[0, :, theirs], wd.at[1]),
        (heads.at[me], hb.at[pool, 0]),
    ]
    loads = [
        pltpu.make_async_copy(source, target, local_sem.at[i])
        for i, (source, target) in enumerate(loads)
    ]
    for load in (loads[7], loads[0]):
        load.start()

    barrier = pltpu.get_barrier_semaphore()
    pl.semaphore_signal(barrier, inc=1, device_id=mate, device_id_type=pl.DeviceIdType.MESH)
    for j in range(1, n):
        pl.semaphore_signal(
            barrier, inc=1, device_id={"dev": flip(me, j)}, device_id_type=pl.DeviceIdType.MESH
        )
    pl.semaphore_wait(barrier, n)

    sends = []
    for j in range(1, n):
        peer = flip(me, j)
        sends.append(
            remote(
                heads.at[peer],
                hb.at[pool, reverse_bits(j, bits)],
                heads_ss.at[j],
                heads_rs.at[j],
                {"dev": peer},
            )
        )
        sends[-1].start()
    for load in loads[1:7]:
        load.start()

    res = residual[...].astype(F32)
    res_own = jnp.where(first, res[:, :half], res[:, half:])
    res_send[...] = jnp.where(first, res[:, half:], res[:, :half])
    swap_res = remote(res_send, res_recv, pool_ss.at[0], pool_rs.at[0], mate)
    swap_res.start()

    loads[7].wait()
    for send in sends:
        send.wait_recv()
    forward = remote(hb.at[pool], hb.at[pool], pool_ss.at[1], pool_rs.at[1], mate)
    forward.start()
    for send in sends:
        send.wait_send()
    loads[0].wait()
    forward.wait()

    wide = hb[...].astype(F32)
    pairs = jnp.concatenate([wide[0, :, :8], wide[1, :, :8]], axis=1).reshape(rows, -1)
    lower = jnp.concatenate([wide[0, :, 8:], wide[1, :, 8:]], axis=1).reshape(rows, -1)
    left = pairs[:, :fold].astype(BF16)
    right = lower[:, :fold].astype(BF16)
    weight = pairs[:, fold : fold + 1] + pairs[:, fold + 1 : fold + 2]
    chunk = quarter // PIECES
    pieces = []
    for k in range(PIECES):
        pieces.append((0, pl.ds(k * chunk, chunk)))
        pieces.append((1, pl.ds(quarter + k * chunk, chunk)))
    near = [(1, 2), (2, 1)]

    def project(c, cols):
        part = jnp.dot(left, wo[:fold, cols], preferred_element_type=F32) + jnp.dot(
            right, wo[fold:, cols], preferred_element_type=F32
        )
        acc[:, :, :, cols] = part.reshape(2, 2, rows // 4, chunk)

    def reduce_rows(prepare):
        def swap(c, stage, send, recv, mask):
            copy = remote(
                send, recv, rs_ss.at[c, stage], rs_rs.at[c, stage], {"dev": flip(me, mask)}
            )
            copy.start()
            return copy

        flying = []
        for c, (side, cols) in enumerate(pieces):
            prepare(c, cols)
            gone = acc[:, 1, :, cols] if side else acc[1, :, :, cols]
            s1[c] = gone.astype(BF16)
            flying.append(swap(c, 0, s1.at[c], r1.at[c], near[side][0]))
        for c, (side, cols) in enumerate(pieces):
            flying[c].wait()
            gone = acc[1, 0, :, cols] if side else acc[0, 1, :, cols]
            s2[c] = (gone + r1[c, 1].astype(F32)).astype(BF16)
            flying[c] = swap(c, 1, s2.at[c], r2.at[c], near[side][1])
            acc[0, 0, :, cols] = acc[0, 0, :, cols] + r1[c, 0].astype(F32)
        keeps = []
        count, slot = rows // 4, 2
        for t in range(tails + 1):
            bit, size = groups[t] if t < tails else (0, 0)
            below = count >> size
            for c, (side, cols) in enumerate(pieces):
                if t == 0:
                    flying[c].wait()
                    keep = acc[0, 0, :, cols] + r2[c].astype(F32)
                else:
                    keep = acc[0, 0, :count, cols]
                    for q, copy in enumerate(flying[c]):
                        copy.wait()
                        keep = keep + tail_recv[t - 1][c, q].astype(F32)
                if t == tails:
                    keeps.append(keep)
                    continue
                flying[c] = []
                for q in range(1, 1 << size):
                    send, recv = tail_send[t].at[c, q - 1], tail_recv[t].at[c, q - 1]
                    send[...] = keep[q * below : (q + 1) * below].astype(BF16)
                    mask = reverse_bits(q, size) << bit
                    flying[c].append(swap(c, slot + q - 1, send, recv, mask))
                acc[0, 0, :below, cols] = keep[:below]
            count, slot = below, slot + (1 << size) - 1
        return jnp.concatenate(keeps[0::2] + keeps[1::2], axis=1)

    attn = reduce_rows(project)
    swap_res.wait()
    res_other = res_recv[...]
    hidden = attn + jnp.concatenate(
        [jnp.where(first, res_own, res_other), jnp.where(first, res_other, res_own)], axis=0
    )
    square = jnp.sum(hidden * hidden, axis=1, keepdims=True)
    sq_send[...] = jnp.broadcast_to(square, sq_send.shape)
    swap_sq = remote(sq_send, sq_recv, pool_ss.at[2], pool_rs.at[2], mate)
    swap_sq.start()
    gains = gain[...].astype(F32)
    gains = jnp.where(first, gains[:, :half], gains[:, half:])
    swap_sq.wait()
    mean_square = (square + sq_recv[:, :1]) / (2 * half)
    normed = (hidden * lax.rsqrt(mean_square + 1e-06) * gains).astype(BF16)
    gathered[0, 0, :ROW] = normed

    def gather(c, stage, view, target, mask):
        copy = remote(view, target, ag_ss.at[c, stage], ag_rs.at[c, stage], {"dev": flip(me, mask)})
        copy.start()
        return copy

    passed = [[] for _ in pieces]

    def pass_on(c, slot, index):
        copy = remote(
            gathered.at[index], other.at[index], pass_ss.at[c, slot], pass_rs.at[c, slot], mate
        )
        copy.start()
        passed[c].append(copy)

    whole = slice(None)
    flying = [[] for _ in pieces]
    count, slot = ROW, 2
    for bit, size in groups[::-1]:
        for c, (side, cols) in enumerate(pieces):
            for copy in flying[c]:
                copy.wait()
            flying[c] = [
                gather(
                    c,
                    slot + q - 1,
                    gathered.at[0, 0, pl.ds(0, count), cols],
                    gathered.at[0, 0, pl.ds(q * count, count), cols],
                    reverse_bits(q, size) << bit,
                )
                for q in range(1, 1 << size)
            ]
        count, slot = count << size, slot + (1 << size) - 1
    for c, (side, cols) in enumerate(pieces):
        for copy in flying[c]:
            copy.wait()
        flying[c] = gather(
            c,
            0,
            gathered.at[0, 0, :, cols],
            gathered.at[1, 0, :, cols] if side else gathered.at[0, 1, :, cols],
            near[side][1],
        )
        pass_on(c, 0, (0, 0, whole, cols))
    for c, (side, cols) in enumerate(pieces):
        flying[c].wait()
        flying[c] = gather(
            c,
            1,
            gathered.at[:, 0, :, cols] if side else gathered.at[0, :, :, cols],
            gathered.at[:, 1, :, cols] if side else gathered.at[1, :, :, cols],
            near[side][0],
        )
        pass_on(c, 1, (1, 0, whole, cols) if side else (0, 1, whole, cols))
    for load in loads[1:7]:
        load.wait()
    gate_proj = jnp.zeros((rows, wg.shape[-1]), F32)
    up_proj = gate_proj
    for c, (side, cols) in enumerate(pieces):
        flying[c].wait()
        pass_on(c, 2, (whole, 1, whole, cols) if side else (1, whole, whole, cols))
        block = gathered[:, :, :, cols].reshape(rows, chunk)
        gate_proj = gate_proj + jnp.dot(block, wg[0, cols], preferred_element_type=F32)
        up_proj = up_proj + jnp.dot(block, wu[0, cols], preferred_element_type=F32)
    for c, (side, cols) in enumerate(pieces):
        for copy in passed[c]:
            copy.wait()
        block = other[:, :, :, cols].reshape(rows, chunk)
        gate_proj = gate_proj + jnp.dot(block, wg[1, cols], preferred_element_type=F32)
        up_proj = up_proj + jnp.dot(block, wu[1, cols], preferred_element_type=F32)
    activated = gate_proj / (1.0 + jnp.exp(-gate_proj)) * up_proj
    activated = (activated * weight).astype(BF16)
    mixes = []
    for c, (side, cols) in enumerate(pieces):
        part = jnp.dot(activated, wd[1, :, cols], preferred_element_type=F32)
        sent = gathered.at[:, :, :, cols]
        sent[...] = part.astype(BF16).reshape(2, 2, rows // 4, chunk)
        mixes.append(remote(sent, pool_recv.at[c], mix_ss.at[c], mix_rs.at[c], mate))
        mixes[-1].start()

    def mix(c, cols):
        part = jnp.dot(activated, wd[0, :, cols], preferred_element_type=F32)
        mixes[c].wait()
        part = part.reshape(2, 2, rows // 4, chunk)
        acc[:, :, :, cols] = part + pool_recv[c].astype(F32)

    total = hidden + reduce_rows(mix)
    out_send[...] = jnp.where(first, total[8:], total[:8])
    swap_out = remote(out_send, out_recv, pool_ss.at[3], pool_rs.at[3], mate)
    swap_out.start()
    kept = jnp.where(first, total[:8], total[8:])
    swap_out.wait()
    come = out_recv[...]
    out[:, :half] = jnp.where(first, kept, come).astype(BF16)
    out[:, half:] = jnp.where(first, come, kept).astype(BF16)


def local(
    residual_in,
    queries,
    key_cache,
    value_cache,
    new_keys,
    new_values,
    lengths,
    out_weight,
    norm_gain,
    expert_ids,
    route_weights,
    w_gate,
    w_up,
    w_down,
):
    rows, model = residual_in.shape
    n = lax.axis_size("dev")
    bits = n.bit_length() - 1
    width = out_weight.shape[0]
    fold = width // 2
    lanes = (fold + 2 + 127) // 128 * 128
    hidden_units = w_gate.shape[2]
    half = model // 2
    heads_out = attend(queries, key_cache, value_cache, new_keys, new_values, lengths)
    blocks = heads_out.reshape(rows, n, 2, fold).transpose(1, 2, 0, 3).reshape(n, 2 * rows, fold)
    named = expert_ids[:, :, None] == jnp.arange(n, dtype=jnp.int32)[None, None, :]
    dense = jnp.sum(jnp.where(named, route_weights[:, :, None], 0.0), axis=1)
    high = lax.reduce_precision(dense, 8, 7)
    weights = jnp.stack([high, dense - high], axis=-1).astype(BF16).transpose(1, 0, 2)
    weights = jnp.pad(weights, ((0, 0), (0, rows), (0, lanes - fold - 2)))
    heads = jnp.concatenate([blocks, weights], axis=2)

    group = n * ROW // 4
    count = 2 * PIECES
    chunk = half // count
    first_step = pltpu.VMEM((count, 2, group, chunk), BF16)
    second_step = pltpu.VMEM((count, group, chunk), BF16)
    tails, below, slots = [], group, 2
    for _, size in grouped(bits):
        below = below >> size
        tails.append(pltpu.VMEM((count, (1 << size) - 1, below, chunk), BF16))
        slots += (1 << size) - 1
    vmem = pl.BlockSpec(memory_space=pltpu.VMEM)
    hbm = pl.BlockSpec(memory_space=pl.ANY)
    dma = pltpu.SemaphoreType.DMA
    return pl.pallas_call(
        functools.partial(layer_kernel, n),
        out_shape=jax.ShapeDtypeStruct((rows, model), BF16),
        in_specs=[hbm, vmem, vmem, hbm, hbm, hbm, hbm],
        out_specs=vmem,
        scratch_shapes=[
            pltpu.VMEM((2, n, ROW, lanes), BF16),
            pltpu.VMEM((width, half), BF16),
            pltpu.VMEM((2, half, hidden_units), BF16),
            pltpu.VMEM((2, half, hidden_units), BF16),
            pltpu.VMEM((2, hidden_units, half), BF16),
            pltpu.VMEM((2, 2, group, half), F32),
            pltpu.VMEM((2, 2, group, half), BF16),
            pltpu.VMEM((2, 2, group, half), BF16),
            pltpu.VMEM((count, 2, 2, group, chunk), BF16),
            pltpu.VMEM((rows, half), F32),
            pltpu.VMEM((rows, half), F32),
            pltpu.VMEM((ROW, 128), F32),
            pltpu.VMEM((ROW, 128), F32),
            pltpu.VMEM((rows, half), F32),
            pltpu.VMEM((rows, half), F32),
            first_step,
            first_step,
            second_step,
            second_step,
            *tails,
            *tails,
            dma((8,)),
            dma((n,)),
            dma((n,)),
            dma((4,)),
            dma((4,)),
            dma((count, slots)),
            dma((count, slots)),
            dma((count, slots)),
            dma((count, slots)),
            dma((count, 3)),
            dma((count, 3)),
            dma((count,)),
            dma((count,)),
        ],
        compiler_params=pltpu.CompilerParams(
            collective_id=0, has_side_effects=True, vmem_limit_bytes=60 * 1024 * 1024
        ),
    )(heads, residual_in, norm_gain.reshape(1, model), out_weight, w_gate, w_up, w_down)


def solution(mesh):
    placed = (
        P(("groups", "pool", "dev"), None),
        P(("groups", "pool", "dev"), None),
        P(("groups", "pool", "dev"), None, None),
        P(("groups", "pool", "dev"), None, None),
        P(("groups", "pool", "dev"), None),
        P(("groups", "pool", "dev"), None),
        P(("groups", "pool", "dev")),
        P("dev", None),
        P(),
        P(("groups", "pool", "dev"), None),
        P(("groups", "pool", "dev"), None),
        P("dev", None, "pool"),
        P("dev", None, "pool"),
        P("dev", "pool", None),
    )
    return jax.shard_map(
        local,
        mesh=mesh,
        in_specs=placed,
        out_specs=P(("groups", "pool", "dev"), None),
        check_vma=False,
    )
```

```python
import functools
import math

import jax
import jax.numpy as jnp
from jax import lax
from jax.experimental import pallas as pl
from jax.experimental.pallas import tpu as pltpu
from jax.sharding import PartitionSpec as P

H = 64
KVH = 4
HD = 128
TOPK = 8


def attend(queries, key_cache, value_cache, new_keys, new_values, lengths):
    rows = queries.shape[0]
    span = key_cache.shape[1]
    group = H // KVH
    query_heads = queries.reshape(rows, KVH, group, HD)
    keys_all = key_cache.reshape(rows, span, KVH, HD)
    values_all = value_cache.reshape(rows, span, KVH, HD)
    scale = 1.0 / math.sqrt(HD)
    scores = (
        jnp.einsum("rkgd,rlkd->rkgl", query_heads, keys_all, preferred_element_type=jnp.float32)
        * scale
    )
    own = (
        jnp.einsum(
            "rkgd,rkd->rkg",
            query_heads,
            new_keys.reshape(rows, KVH, HD),
            preferred_element_type=jnp.float32,
        )
        * scale
    )
    valid = (jnp.arange(span, dtype=jnp.int32)[None, :] < lengths[:, None])[:, None, None, :]
    scores = jnp.where(valid, scores, -1e30)
    top = jnp.maximum(jnp.max(scores, axis=-1), own)
    weights = jnp.where(valid, jnp.exp(scores - top[..., None]), 0.0)
    own_weight = jnp.exp(own - top)
    total = jnp.sum(weights, axis=-1) + own_weight
    weights = (weights / total[..., None]).astype(jnp.bfloat16)
    own_weight = (own_weight / total).astype(jnp.bfloat16)
    mixed = jnp.einsum("rkgl,rlkd->rkgd", weights, values_all, preferred_element_type=jnp.float32)
    mixed = mixed + own_weight.astype(jnp.float32)[..., None] * new_values.reshape(
        rows, KVH, 1, HD
    ).astype(jnp.float32)
    return mixed.reshape(rows, H * HD).astype(jnp.bfloat16)


F32 = jnp.float32
BF16 = jnp.bfloat16
ROW = 16
PIECES = 2


def flip(index, mask):
    for bit in range(mask.bit_length()):
        if (mask >> bit) & 1:
            index = index + (1 << bit) * (1 - 2 * ((index // (1 << bit)) % 2))
    return index


def reverse_bits(value, bits):
    return sum(((value >> bit) & 1) << (bits - 1 - bit) for bit in range(bits))


def grouped(bits):
    return [(bit, min(2, bits - bit)) for bit in range(2, bits, 2)]


def layer_kernel(n, *refs):
    bits = n.bit_length() - 1
    groups = grouped(bits)
    tails = len(groups)
    refs = list(refs)

    def take(count):
        taken = refs[:count]
        del refs[:count]
        return taken

    heads, residual, gain, wo_hbm, wg_hbm, wu_hbm, wd_hbm, out = take(8)
    hb, wo, wg, wu, wd, acc, gathered, other, pool_recv = take(9)
    res_send, res_recv, sq_send, sq_recv, out_send, out_recv = take(6)
    s1, r1, s2, r2 = take(4)
    tail_send, tail_recv = take(tails), take(tails)
    local_sem, heads_ss, heads_rs, pool_ss, pool_rs, rs_ss, rs_rs, ag_ss, ag_rs = take(9)
    pass_ss, pass_rs, mix_ss, mix_rs = take(4)

    me = lax.axis_index("dev")
    pool = lax.axis_index("pool")
    mate = {"pool": 1 - pool}
    first = pool == 0
    half = acc.shape[-1]
    quarter = half // 2
    width = wo.shape[0]
    fold = width // 2
    rows = n * ROW

    def remote(source, target, send_sem, recv_sem, device):
        return pltpu.make_async_remote_copy(
            src_ref=source,
            dst_ref=target,
            send_sem=send_sem,
            recv_sem=recv_sem,
            device_id=device,
            device_id_type=pl.DeviceIdType.MESH,
        )

    mine = pl.ds(pl.multiple_of(pool * half, half), half)
    theirs = pl.ds(pl.multiple_of((1 - pool) * half, half), half)
    loads = [
        (wo_hbm.at[:, mine], wo),
        (wg_hbm.at[0, mine], wg.at[0]),
        (wg_hbm.at[0, theirs], wg.at[1]),
        (wu_hbm.at[0, mine], wu.at[0]),
        (wu_hbm.at[0, theirs], wu.at[1]),
        (wd_hbm.at[0, :, mine], wd.at[0]),
        (wd_hbm.at[0, :, theirs], wd.at[1]),
        (heads.at[me], hb.at[pool, 0]),
    ]
    loads = [
        pltpu.make_async_copy(source, target, local_sem.at[i])
        for i, (source, target) in enumerate(loads)
    ]
    for load in (loads[7], loads[0]):
        load.start()

    barrier = pltpu.get_barrier_semaphore()
    pl.semaphore_signal(barrier, inc=1, device_id=mate, device_id_type=pl.DeviceIdType.MESH)
    for j in range(1, n):
        pl.semaphore_signal(
            barrier, inc=1, device_id={"dev": flip(me, j)}, device_id_type=pl.DeviceIdType.MESH
        )
    pl.semaphore_wait(barrier, n)

    sends = []
    for j in range(1, n):
        peer = flip(me, j)
        sends.append(
            remote(
                heads.at[peer],
                hb.at[pool, reverse_bits(j, bits)],
                heads_ss.at[j],
                heads_rs.at[j],
                {"dev": peer},
            )
        )
        sends[-1].start()
    for load in loads[1:7]:
        load.start()

    res = residual[...].astype(F32)
    res_own = jnp.where(first, res[:, :half], res[:, half:])
    res_send[...] = jnp.where(first, res[:, half:], res[:, :half])
    swap_res = remote(res_send, res_recv, pool_ss.at[0], pool_rs.at[0], mate)
    swap_res.start()

    loads[7].wait()
    for send in sends:
        send.wait_recv()
    forward = remote(hb.at[pool], hb.at[pool], pool_ss.at[1], pool_rs.at[1], mate)
    forward.start()
    loads[0].wait()
    forward.wait()

    wide = hb[...].astype(F32)
    pairs = jnp.concatenate([wide[0, :, :8], wide[1, :, :8]], axis=1).reshape(rows, -1)
    lower = jnp.concatenate([wide[0, :, 8:], wide[1, :, 8:]], axis=1).reshape(rows, -1)
    left = pairs[:, :fold].astype(BF16)
    right = lower[:, :fold].astype(BF16)
    weight = pairs[:, fold : fold + 1] + pairs[:, fold + 1 : fold + 2]
    chunk = quarter // PIECES
    pieces = []
    for k in range(PIECES):
        pieces.append((0, pl.ds(k * chunk, chunk)))
        pieces.append((1, pl.ds(quarter + k * chunk, chunk)))
    near = [(1, 2), (2, 1)]

    def project(c, cols):
        part = jnp.dot(left, wo[:fold, cols], preferred_element_type=F32) + jnp.dot(
            right, wo[fold:, cols], preferred_element_type=F32
        )
        acc[:, :, :, cols] = part.reshape(2, 2, rows // 4, chunk)

    def reduce_rows(prepare):
        def swap(c, stage, send, recv, mask):
            copy = remote(
                send, recv, rs_ss.at[c, stage], rs_rs.at[c, stage], {"dev": flip(me, mask)}
            )
            copy.start()
            return copy

        flying = []
        for c, (side, cols) in enumerate(pieces):
            prepare(c, cols)
            gone = acc[:, 1, :, cols] if side else acc[1, :, :, cols]
            s1[c] = gone.astype(BF16)
            flying.append(swap(c, 0, s1.at[c], r1.at[c], near[side][0]))
        for c, (side, cols) in enumerate(pieces):
            flying[c].wait()
            gone = acc[1, 0, :, cols] if side else acc[0, 1, :, cols]
            s2[c] = (gone + r1[c, 1].astype(F32)).astype(BF16)
            flying[c] = swap(c, 1, s2.at[c], r2.at[c], near[side][1])
            acc[0, 0, :, cols] = acc[0, 0, :, cols] + r1[c, 0].astype(F32)
        keeps = []
        count, slot = rows // 4, 2
        for t in range(tails + 1):
            bit, size = groups[t] if t < tails else (0, 0)
            below = count >> size
            for c, (side, cols) in enumerate(pieces):
                if t == 0:
                    flying[c].wait()
                    keep = acc[0, 0, :, cols] + r2[c].astype(F32)
                else:
                    keep = acc[0, 0, :count, cols]
                    for q, copy in enumerate(flying[c]):
                        copy.wait()
                        keep = keep + tail_recv[t - 1][c, q].astype(F32)
                if t == tails:
                    keeps.append(keep)
                    continue
                flying[c] = []
                for q in range(1, 1 << size):
                    send, recv = tail_send[t].at[c, q - 1], tail_recv[t].at[c, q - 1]
                    send[...] = keep[q * below : (q + 1) * below].astype(BF16)
                    mask = reverse_bits(q, size) << bit
                    flying[c].append(swap(c, slot + q - 1, send, recv, mask))
                acc[0, 0, :below, cols] = keep[:below]
            count, slot = below, slot + (1 << size) - 1
        return jnp.concatenate(keeps[0::2] + keeps[1::2], axis=1)

    attn = reduce_rows(project)
    for send in sends:
        send.wait_send()
    swap_res.wait()
    res_other = res_recv[...]
    hidden = attn + jnp.concatenate(
        [jnp.where(first, res_own, res_other), jnp.where(first, res_other, res_own)], axis=0
    )
    square = jnp.sum(hidden * hidden, axis=1, keepdims=True)
    sq_send[...] = jnp.broadcast_to(square, sq_send.shape)
    swap_sq = remote(sq_send, sq_recv, pool_ss.at[2], pool_rs.at[2], mate)
    swap_sq.start()
    gains = gain[...].astype(F32).reshape(1, 2 * half)
    gains = jnp.where(first, gains[:, :half], gains[:, half:])
    swap_sq.wait()
    mean_square = (square + sq_recv[:, :1]) / (2 * half)
    normed = (hidden * lax.rsqrt(mean_square + 1e-06) * gains).astype(BF16)
    gathered[0, 0, :ROW] = normed

    def gather(c, stage, view, target, mask):
        copy = remote(view, target, ag_ss.at[c, stage], ag_rs.at[c, stage], {"dev": flip(me, mask)})
        copy.start()
        return copy

    passed = [[] for _ in pieces]

    def pass_on(c, slot, index):
        copy = remote(
            gathered.at[index], other.at[index], pass_ss.at[c, slot], pass_rs.at[c, slot], mate
        )
        copy.start()
        passed[c].append(copy)

    whole = slice(None)
    flying = [[] for _ in pieces]
    count, slot = ROW, 2
    for bit, size in groups[::-1]:
        for c, (side, cols) in enumerate(pieces):
            for copy in flying[c]:
                copy.wait()
            flying[c] = [
                gather(
                    c,
                    slot + q - 1,
                    gathered.at[0, 0, pl.ds(0, count), cols],
                    gathered.at[0, 0, pl.ds(q * count, count), cols],
                    reverse_bits(q, size) << bit,
                )
                for q in range(1, 1 << size)
            ]
        count, slot = count << size, slot + (1 << size) - 1
    for c, (side, cols) in enumerate(pieces):
        for copy in flying[c]:
            copy.wait()
        flying[c] = gather(
            c,
            0,
            gathered.at[0, 0, :, cols],
            gathered.at[1, 0, :, cols] if side else gathered.at[0, 1, :, cols],
            near[side][1],
        )
        pass_on(c, 0, (0, 0, whole, cols))
    for c, (side, cols) in enumerate(pieces):
        flying[c].wait()
        flying[c] = gather(
            c,
            1,
            gathered.at[:, 0, :, cols] if side else gathered.at[0, :, :, cols],
            gathered.at[:, 1, :, cols] if side else gathered.at[1, :, :, cols],
            near[side][0],
        )
        pass_on(c, 1, (1, 0, whole, cols) if side else (0, 1, whole, cols))
    for load in loads[1:7]:
        load.wait()
    gate_proj = jnp.zeros((rows, wg.shape[-1]), F32)
    up_proj = gate_proj
    for c, (side, cols) in enumerate(pieces):
        flying[c].wait()
        pass_on(c, 2, (whole, 1, whole, cols) if side else (1, whole, whole, cols))
        block = gathered[:, :, :, cols].reshape(rows, chunk)
        gate_proj = gate_proj + jnp.dot(block, wg[0, cols], preferred_element_type=F32)
        up_proj = up_proj + jnp.dot(block, wu[0, cols], preferred_element_type=F32)
    for c, (side, cols) in enumerate(pieces):
        for copy in passed[c]:
            copy.wait()
        block = other[:, :, :, cols].reshape(rows, chunk)
        gate_proj = gate_proj + jnp.dot(block, wg[1, cols], preferred_element_type=F32)
        up_proj = up_proj + jnp.dot(block, wu[1, cols], preferred_element_type=F32)
    activated = gate_proj / (1.0 + jnp.exp(-gate_proj)) * up_proj
    activated = (activated * weight).astype(BF16)
    mixes = []
    for c, (side, cols) in enumerate(pieces):
        part = jnp.dot(activated, wd[1, :, cols], preferred_element_type=F32)
        sent = gathered.at[:, :, :, cols]
        sent[...] = part.astype(BF16).reshape(2, 2, rows // 4, chunk)
        mixes.append(remote(sent, pool_recv.at[c], mix_ss.at[c], mix_rs.at[c], mate))
        mixes[-1].start()

    def mix(c, cols):
        part = jnp.dot(activated, wd[0, :, cols], preferred_element_type=F32)
        mixes[c].wait()
        part = part.reshape(2, 2, rows // 4, chunk)
        acc[:, :, :, cols] = part + pool_recv[c].astype(F32)

    total = hidden + reduce_rows(mix)
    out_send[...] = jnp.where(first, total[8:], total[:8])
    swap_out = remote(out_send, out_recv, pool_ss.at[3], pool_rs.at[3], mate)
    swap_out.start()
    kept = jnp.where(first, total[:8], total[8:])
    swap_out.wait()
    come = out_recv[...]
    out[:, :half] = jnp.where(first, kept, come).astype(BF16)
    out[:, half:] = jnp.where(first, come, kept).astype(BF16)


def local(
    residual_in,
    queries,
    key_cache,
    value_cache,
    new_keys,
    new_values,
    lengths,
    out_weight,
    norm_gain,
    expert_ids,
    route_weights,
    w_gate,
    w_up,
    w_down,
):
    rows, model = residual_in.shape
    n = lax.axis_size("dev")
    bits = n.bit_length() - 1
    width = out_weight.shape[0]
    fold = width // 2
    lanes = (fold + 2 + 127) // 128 * 128
    hidden_units = w_gate.shape[2]
    half = model // 2
    heads_out = attend(queries, key_cache, value_cache, new_keys, new_values, lengths)
    blocks = heads_out.reshape(rows, n, 2, fold).transpose(1, 2, 0, 3).reshape(n, 2 * rows, fold)
    named = expert_ids[:, :, None] == jnp.arange(n, dtype=jnp.int32)[None, None, :]
    dense = jnp.sum(jnp.where(named, route_weights[:, :, None], 0.0), axis=1)
    high = lax.reduce_precision(dense, 8, 7)
    weights = jnp.stack([high, dense - high], axis=-1).astype(BF16).transpose(1, 0, 2)
    weights = jnp.pad(weights, ((0, 0), (0, rows), (0, lanes - fold - 2)))
    heads = jnp.concatenate([blocks, weights], axis=2)

    group = n * ROW // 4
    count = 2 * PIECES
    chunk = half // count
    first_step = pltpu.VMEM((count, 2, group, chunk), BF16)
    second_step = pltpu.VMEM((count, group, chunk), BF16)
    tails, below, slots = [], group, 2
    for _, size in grouped(bits):
        below = below >> size
        tails.append(pltpu.VMEM((count, (1 << size) - 1, below, chunk), BF16))
        slots += (1 << size) - 1
    vmem = pl.BlockSpec(memory_space=pltpu.VMEM)
    hbm = pl.BlockSpec(memory_space=pl.ANY)
    dma = pltpu.SemaphoreType.DMA
    return pl.pallas_call(
        functools.partial(layer_kernel, n),
        out_shape=jax.ShapeDtypeStruct((rows, model), BF16),
        in_specs=[hbm, vmem, vmem, hbm, hbm, hbm, hbm],
        out_specs=vmem,
        scratch_shapes=[
            pltpu.VMEM((2, n, ROW, lanes), BF16),
            pltpu.VMEM((width, half), BF16),
            pltpu.VMEM((2, half, hidden_units), BF16),
            pltpu.VMEM((2, half, hidden_units), BF16),
            pltpu.VMEM((2, hidden_units, half), BF16),
            pltpu.VMEM((2, 2, group, half), F32),
            pltpu.VMEM((2, 2, group, half), BF16),
            pltpu.VMEM((2, 2, group, half), BF16),
            pltpu.VMEM((count, 2, 2, group, chunk), BF16),
            pltpu.VMEM((rows, half), F32),
            pltpu.VMEM((rows, half), F32),
            pltpu.VMEM((ROW, 128), F32),
            pltpu.VMEM((ROW, 128), F32),
            pltpu.VMEM((rows, half), F32),
            pltpu.VMEM((rows, half), F32),
            first_step,
            first_step,
            second_step,
            second_step,
            *tails,
            *tails,
            dma((8,)),
            dma((n,)),
            dma((n,)),
            dma((4,)),
            dma((4,)),
            dma((count, slots)),
            dma((count, slots)),
            dma((count, slots)),
            dma((count, slots)),
            dma((count, 3)),
            dma((count, 3)),
            dma((count,)),
            dma((count,)),
        ],
        compiler_params=pltpu.CompilerParams(
            collective_id=0, has_side_effects=True, vmem_limit_bytes=60 * 1024 * 1024
        ),
    )(heads, residual_in, norm_gain, out_weight, w_gate, w_up, w_down)


def solution(mesh):
    placed = (
        P(("groups", "pool", "dev"), None),
        P(("groups", "pool", "dev"), None),
        P(("groups", "pool", "dev"), None, None),
        P(("groups", "pool", "dev"), None, None),
        P(("groups", "pool", "dev"), None),
        P(("groups", "pool", "dev"), None),
        P(("groups", "pool", "dev")),
        P("dev", None),
        P(),
        P(("groups", "pool", "dev"), None),
        P(("groups", "pool", "dev"), None),
        P("dev", None, "pool"),
        P("dev", None, "pool"),
        P("dev", "pool", None),
    )
    return jax.shard_map(
        local,
        mesh=mesh,
        in_specs=placed,
        out_specs=P(("groups", "pool", "dev"), None),
        check_vma=False,
    )
```
